32 devices in a mesh: grp: 1, seq: 8 (over y, x, core), ep: 4 (over z).
Axes of the slice: x: 2, y: 2, z: 4, core: 2. Of those that a mesh axis runs over, the one named last changes fastest.
Arguments:
- queries: bfloat16 [256, 64, 128], P(('grp', 'seq', 'ep')), may hold values from -110 to 110
- key_codes: bfloat16 [4352, 4, 128], P(('grp', 'seq')), may hold values from -4.5 to 4.5
- quantized_value_cache: bfloat16 [4352, 4, 128], P(('grp', 'seq')), may hold values from -4.5 to 4.5
- key_scale: bfloat16 [4352, 4], P(('grp', 'seq')), may hold values from 0.3 to 3
- value_code_scale: bfloat16 [4352, 4], P(('grp', 'seq')), may hold values from 0.29882812 to 3
- out_weight: bfloat16 [8192, 4096], P('seq', 'ep'), may hold values from -0.0625 to 0.0625
- residual: bfloat16 [256, 4096], P(('grp', 'seq', 'ep')), may hold values from -2.5 to 2.5
- norm_gain: float32 [4096], replicated, may hold values from 0.1 to 1.9
- route_ids: int32 [256, 8], P(('grp', 'seq', 'ep')), may hold values from 0 to 15, all different within a row; in each aligned block of 8 rows (0 to 7, 8 to 15, ...) at most 8 rows name the same one
- route_weight: float32 [256, 8], P(('grp', 'seq', 'ep')), may hold values from 0.1 to 1
- w_gate: bfloat16 [4096, 12288], P(None, ('seq', 'ep')), may hold values from -0.09375 to 0.09375
- w_up: bfloat16 [4096, 12288], P(None, ('seq', 'ep')), may hold values from -0.09375 to 0.09375
- w_down: bfloat16 [12288, 4096], P(('seq', 'ep')), may hold values from -0.21875 to 0.21875
Outputs:
- hidden_state: bfloat16 [256, 4096], P(('grp', 'seq', 'ep'))
- expert_out: bfloat16 [256, 4096], P(('grp', 'seq', 'ep'))
The draws below stay inside these ranges and needn't reach their ends.
Inputs may be any that keep to these rules, and one draw needn't show every extreme that they name: `route_ids`: each token names 8 different experts; in the 8 tokens of one device (aligned blocks) no expert is named by more than 8 routes.
All inputs are finite; a program needn't handle non-finite values.
Results may differ from the reference program's by a relative error of at most 0.025.
Values may be sent and summed in bfloat16 or wider, within the bound.
A program may use at most 64 MiB of HBM per device.

```python
import math
import jax
import jax.numpy as jnp
import numpy as np
from jax import lax

D = 4096
QUERY_HEADS = 64
KEY_VALUE_HEADS = 4
HEAD_SIZE = 128
TOPK = 8
EH = 768
TOK_DEV = 8
E = 16
CAP = 8
S = 256
CACHE_LENGTH = 4352


def drawn_draw(key):
    query_key, key_code_seed, key_scale_seed = jax.random.split(key, 3)
    value_code_draw = jnp.clip(jax.random.normal(key_code_seed, (CACHE_LENGTH, KEY_VALUE_HEADS, HEAD_SIZE), jnp.float32), -4.5, 4.5)
    scale_arrays = jnp.exp(jax.random.uniform(key_scale_seed, (CACHE_LENGTH, KEY_VALUE_HEADS), jnp.float32, jnp.log(0.3), jnp.log(3.0)))
    query_values = jnp.clip(jax.random.normal(query_key, (S, QUERY_HEADS, HEAD_SIZE), jnp.float32), -6.0, 6.0)
    return (query_values, value_code_draw, scale_arrays)


def draw_queries(key, part):
    values = drawn_draw(key)
    return values[0].astype(jnp.bfloat16)


def draw_key_codes(key, part):
    values = drawn_draw(key)
    return values[1].astype(jnp.bfloat16)


def draw_key_scale(key, part):
    values = drawn_draw(key)
    return values[2].astype(jnp.bfloat16)


def levels(key, extent, shards, least, top_value):
    level = 1.0
    for axis_at, shards_of in shards:
        steps = jax.random.uniform(jax.random.fold_in(jax.random.fold_in(key, 6), axis_at), (shards_of,), jnp.float32, least / len(shards), top_value / len(shards))
        level = level * jnp.repeat(jnp.exp(steps), extent[axis_at] // shards_of).reshape((-1,) + (1,) * (len(extent) - 1 - axis_at))
    return level


def deal_out(rng, own, number, rows, count, top, reach, lean):
    ranking = jax.random.permutation(rng, count)
    heavy_load, common = load_shares(count, rows * top, reach, lean, True), load_shares(count, rows * top, reach, lean, False)
    places = jnp.arange(count)

    def named(sizes, turn):
        used = int((sizes > 0).sum())
        fixed = max(1, used // 4)
        passed = fixed + (places - fixed + turn * (used - fixed)) % max(1, count - fixed)
        return jnp.zeros((count,), jnp.int32).at[ranking[jnp.where(places < fixed, places, passed)]].set(jnp.asarray(sizes, jnp.int32))

    sizes = jnp.where(number % 4 == 0, named(heavy_load, number // 4), named(common, number - number // 4 - 1))
    mixed = jax.random.permutation(jax.random.fold_in(own, 3), count)
    giver, receiver = mixed[0:count // 2 * 2:2], mixed[1:count // 2 * 2:2]
    margin = jnp.minimum(sizes[giver] - 1, reach - sizes[receiver]) // 2
    margin = jnp.where((giver == ranking[0]) | (receiver == ranking[0]) | (sizes[receiver] == 0), 0, jnp.maximum(margin, 0))
    passed = jax.random.randint(jax.random.fold_in(own, 4), (count // 2,), 0, 1 << 20) % (margin + 1)
    sizes = sizes.at[giver].add(-passed).at[receiver].add(passed)
    items = jnp.searchsorted(jnp.cumsum(sizes), jnp.arange(rows * top), side="right").astype(jnp.int32)
    grid = items.reshape(top, rows).T
    grid = grid[jax.random.permutation(jax.random.fold_in(own, 1), rows)]
    turn = jax.random.randint(jax.random.fold_in(own, 2), (rows, 1), 0, top)
    return jnp.take_along_axis(grid, (jnp.arange(top)[None, :] + turn) % top, axis=1)


def load_shares(number_of, total, reach, slope, full):
    weights = [(1 << 20) // math.isqrt(standing ** slope) + 1 for standing in range(1, number_of + 1)]
    largest = reach if full else min(reach, max(-(-total // number_of), total * weights[0] // sum(weights)))
    least = 1 if total - largest >= number_of - 1 else 0
    given, spare = [largest] + [least] * (number_of - 1), total - largest - least * (number_of - 1)
    while spare > 0:
        free = [i for i in range(1, number_of) if given[i] < largest] or [i for i in range(1, number_of) if given[i] < reach]
        whole, remaining = sum([weights[i] for i in free]), spare
        for i in free:
            addition = min(reach - given[i], max(1, remaining * weights[i] // whole), spare)
            given[i] = given[i] + addition
            spare = spare - addition
    return np.array(given)


def scatter_about(stream_key, dims, scale, bound, pieces=(), held_as=jnp.bfloat16):
    drawn = jax.random.normal(stream_key, dims, jnp.float32) * scale
    if len(pieces) > 0:
        drawn = levels(stream_key, dims, pieces, -0.22, 0.18) * drawn
    return jnp.clip(drawn, min=-bound, max=bound).astype(held_as)


def setup_inputs(seed: int = 0, part: int = 0) -> dict:
    splits = jax.random.split(jax.random.key(seed), 14)
    part_splits = jax.random.split(jax.random.fold_in(splits[13], part), 14)
    queries = draw_queries(jax.random.fold_in(jax.random.fold_in(splits[13], part), 71), part)
    key_codes = draw_key_codes(jax.random.fold_in(jax.random.fold_in(splits[13], part), 71), part)
    quantized_value_cache = scatter_about(part_splits[2], (CACHE_LENGTH, KEY_VALUE_HEADS, HEAD_SIZE), 1.0, 4.5, ((0, 8),))
    key_scale = draw_key_scale(jax.random.fold_in(jax.random.fold_in(splits[13], part), 71), part)
    value_code_scale = jnp.clip(jnp.exp(math.log(3.0) - 2.306499 * jax.random.uniform(part_splits[4], (CACHE_LENGTH, KEY_VALUE_HEADS), jnp.float32) ** levels(part_splits[4], (CACHE_LENGTH, KEY_VALUE_HEADS), ((0, 8),), -0.2, 0.2)), 0.29882812, 3.0).astype(jnp.bfloat16)
    out_weight = scatter_about(splits[5], (QUERY_HEADS * HEAD_SIZE, D), (QUERY_HEADS * HEAD_SIZE) ** -0.5, 0.0625, ((0, 8), (1, 4)))
    residual = scatter_about(part_splits[6], (S, D), 0.3, 2.5, ((0, 32),))
    norm_gain = jnp.clip(1.0 + 0.18 * jax.random.normal(splits[7], (D,), jnp.float32), 0.1, 1.9)
    route_ids_keys = jax.random.split(jax.random.fold_in(part_splits[8], 1), S // TOK_DEV)
    route_ids_turns = jax.random.permutation(jax.random.fold_in(part_splits[8], 3), S // TOK_DEV)
    route_ids = jax.vmap(lambda own, number: deal_out(jax.random.fold_in(part_splits[8], 2), own, number, TOK_DEV, E, TOPK, CAP, 1))(route_ids_keys, route_ids_turns).reshape((S, TOPK))
    route_weight = jnp.clip(jnp.exp(math.log(1.0) - 2.3025851 * jax.random.uniform(part_splits[9], (S, TOPK), jnp.float32) ** levels(part_splits[9], (S, TOPK), ((0, 32),), -0.2, 0.2)), 0.1, 1.0)
    w_gate = scatter_about(splits[10], (D, E * EH), D ** -0.5, 0.09375, ((1, 32),))
    w_up = scatter_about(splits[11], (D, E * EH), D ** -0.5, 0.09375, ((1, 32),))
    w_down = scatter_about(splits[12], (E * EH, D), EH ** -0.5, 0.21875, ((0, 32),))
    return {"queries": queries, "key_codes": key_codes, "quantized_value_cache": quantized_value_cache, "key_scale": key_scale, "value_code_scale": value_code_scale, "out_weight": out_weight, "residual": residual, "norm_gain": norm_gain, "route_ids": route_ids, "route_weight": route_weight, "w_gate": w_gate, "w_up": w_up, "w_down": w_down}


eps_norm = 1e-06

def attention_heads(queries, key_codes, quantized_value_cache, key_scale, value_code_scale):
    window_len = queries.shape[0]
    total_len = key_codes.shape[0]
    prefix_len = total_len - window_len
    query_pos = prefix_len + jnp.arange(window_len, dtype=jnp.int32)
    key_pos = jnp.arange(total_len, dtype=jnp.int32)
    visible = key_pos[None, :] <= query_pos[:, None]
    inverse = 1.0 / math.sqrt(HEAD_SIZE)
    heads_per_group = QUERY_HEADS // KEY_VALUE_HEADS

    def one_head(head_index):
        group_index = head_index // heads_per_group
        query_head = lax.dynamic_index_in_dim(queries, head_index, 1, keepdims=False)
        key_head = lax.dynamic_index_in_dim(key_codes, group_index, 1, keepdims=False)
        value_head = lax.dynamic_index_in_dim(quantized_value_cache, group_index, 1, keepdims=False)
        scale_keys = lax.dynamic_index_in_dim(key_scale, group_index, 1, keepdims=False).astype(jnp.float32)
        scale_values = lax.dynamic_index_in_dim(value_code_scale, group_index, 1, keepdims=False).astype(jnp.float32)
        scores = jnp.dot(query_head, key_head.T, preferred_element_type=jnp.float32)
        scores = scores * (scale_keys[None, :] * inverse)
        scores = jnp.where(visible, scores, -jnp.inf)
        row_max = lax.optimization_barrier(jnp.max(scores, axis=1, keepdims=True))
        exp_scores = jnp.exp(scores - row_max)
        row_sum = lax.optimization_barrier(jnp.sum(exp_scores, axis=1, keepdims=True))
        weighted = (exp_scores * scale_values[None, :]).astype(jnp.bfloat16)
        mixed = jnp.dot(weighted, value_head, preferred_element_type=jnp.float32) / row_sum
        return mixed.astype(jnp.bfloat16)
    per_head = lax.map(one_head, jnp.arange(QUERY_HEADS, dtype=jnp.int32))
    return jnp.transpose(per_head, (1, 0, 2)).reshape(window_len, QUERY_HEADS * HEAD_SIZE)

def expert_answers(normed, route_ids, w_gate, w_up, w_down):
    window_len = normed.shape[0]
    block_count = window_len // TOK_DEV
    route_len = TOK_DEV * TOPK
    flat_ids = route_ids.reshape(block_count, route_len)
    onehot = (flat_ids[:, :, None] == jnp.arange(E, dtype=jnp.int32)[None, None, :]).astype(jnp.int32)
    slot_index = lax.optimization_barrier(jnp.sum((jnp.cumsum(onehot, axis=1) - onehot) * onehot, axis=2))
    expected_output = (flat_ids * CAP + slot_index).astype(jnp.int32)
    token_rows = jnp.repeat(normed.reshape(block_count, TOK_DEV, D), TOPK, axis=1)
    block_idx = jnp.repeat(jnp.arange(block_count, dtype=jnp.int32)[:, None], route_len, axis=1)
    buffers = jnp.zeros((block_count, E * CAP, D), normed.dtype).at[block_idx, expected_output].set(token_rows)
    by_expert = buffers.reshape(block_count, E, CAP, D).transpose(1, 0, 2, 3).reshape(E, block_count * CAP, D)
    half_width = EH // 2

    def one_expert(inputs):
        rows_in, expert_index = inputs
        start_col = expert_index * EH
        gate_cols = lax.dynamic_slice_in_dim(w_gate, start_col, EH, 1)
        up_cols = lax.dynamic_slice_in_dim(w_up, start_col, EH, 1)
        down_rows = lax.dynamic_slice_in_dim(w_down, start_col, EH, 0)
        gate_val = jnp.dot(rows_in, gate_cols, preferred_element_type=jnp.float32)
        up_val = jnp.dot(rows_in, up_cols, preferred_element_type=jnp.float32)
        active = (jax.nn.silu(gate_val) * up_val).astype(jnp.bfloat16)
        lower_half = jnp.dot(active[:, :half_width], down_rows[:half_width], preferred_element_type=jnp.float32).astype(jnp.bfloat16)
        upper_half = jnp.dot(active[:, half_width:], down_rows[half_width:], preferred_element_type=jnp.float32).astype(jnp.bfloat16)
        return (lower_half.astype(jnp.float32) + upper_half.astype(jnp.float32)).astype(jnp.bfloat16)
    answers = lax.map(one_expert, (by_expert, jnp.arange(E, dtype=jnp.int32)))
    returned = answers.reshape(E, block_count, CAP, D).transpose(1, 0, 2, 3).reshape(block_count, E * CAP, D)
    picked = returned[block_idx, expected_output]
    return picked.reshape(window_len, TOPK, D)

def reference(queries, key_codes, quantized_value_cache, key_scale, value_code_scale, out_weight, residual, norm_gain, route_ids, route_weight, w_gate, w_up, w_down):
    attention = attention_heads(queries, key_codes, quantized_value_cache, key_scale, value_code_scale)
    summed = residual.astype(jnp.float32) + jnp.dot(attention, out_weight, preferred_element_type=jnp.float32)
    hidden_state = summed.astype(jnp.bfloat16)
    hidden_wide = hidden_state.astype(jnp.float32)
    mean_square = lax.optimization_barrier(jnp.mean(hidden_wide * hidden_wide, axis=1, keepdims=True))
    normed = (hidden_wide * lax.rsqrt(mean_square + eps_norm) * norm_gain[None, :]).astype(jnp.bfloat16)
    picked = expert_answers(normed, route_ids, w_gate, w_up, w_down)
    mix_weight = route_weight / lax.optimization_barrier(jnp.sum(route_weight, axis=1, keepdims=True))
    expert_out = lax.optimization_barrier(jnp.sum(mix_weight[:, :, None] * picked.astype(jnp.float32), axis=1)).astype(jnp.bfloat16)
    return (hidden_state, expert_out)
```

```python
import functools
import math

import jax
import jax.numpy as jnp
from jax import lax
from jax.experimental import pallas as pl
from jax.experimental.pallas import tpu as pltpu
from jax.sharding import PartitionSpec as P

eps_norm = 1e-06
MESH = pl.DeviceIdType.MESH
hidden_score = -1e30


def device_at(seq_pos, ep_pos):
    return {"seq": seq_pos, "ep": ep_pos}


def remote(src, dst, send_sem, recv_sem, seq_pos, ep_pos):
    return pltpu.make_async_remote_copy(
        src_ref=src,
        dst_ref=dst,
        send_sem=send_sem,
        recv_sem=recv_sem,
        device_id=device_at(seq_pos, ep_pos),
        device_id_type=MESH,
    )


def attention_kernel(
    n_seq,
    n_ep,
    copies,
    tokens,
    heads,
    prefix_len,
    q_ref,
    kv_ref,
    scale_ref,
    out_ref,
    q_all,
    kv_all,
    scale_all,
    top,
    total,
    acc,
    wide,
    q_send,
    q_recv,
    kv_send,
    kv_recv,
    scale_send,
    scale_recv,
    own_sem,
):
    me = lax.axis_index("seq")
    zed = lax.axis_index("ep")
    groups = n_seq // copies
    group = me // copies
    member = me % copies
    head_dim = q_ref.shape[2]
    local_len = scale_ref.shape[2]
    rows_each = tokens * heads

    barrier = pltpu.get_barrier_semaphore()
    for step in range(1, n_seq):
        pl.semaphore_signal(
            barrier,
            inc=1,
            device_id=device_at((me + step) % n_seq, zed),
            device_id_type=MESH,
        )
    own = pltpu.make_async_copy(q_ref.at[me], q_all.at[me], own_sem)
    own.start()
    top[...] = jnp.full_like(top, hidden_score)
    total[...] = jnp.zeros_like(total)
    acc[...] = jnp.zeros_like(acc)
    pl.semaphore_wait(barrier, n_seq - 1)

    pending = []
    q_copies = []
    for step in range(1, n_seq):
        to = (me + step) % n_seq
        c = remote(q_ref.at[to], q_all.at[me], q_send.at[step], q_recv.at[step], to, zed)
        c.start()
        q_copies.append(c)

    def send_kv(kv_src, scale_src, i, q, to):
        a = remote(kv_src, kv_all.at[i, q], kv_send.at[i, q], kv_recv.at[i, q], to, zed)
        b = remote(
            scale_src, scale_all.at[i, q], scale_send.at[i, q], scale_recv.at[i, q], to, zed
        )
        a.start()
        b.start()
        pending.append((a, b))
        return (a, b)

    arrivals = {}
    for i in range(1, groups):
        goal = (group + i) % groups
        arrivals[i, 0] = send_kv(
            kv_ref.at[goal], scale_ref.at[goal], i, 0, goal * copies + member
        )
    for q in range(1, copies):
        arrivals[0, q] = send_kv(
            kv_ref.at[group],
            scale_ref.at[group],
            0,
            q,
            group * copies + (member + q) % copies,
        )

    own.wait()
    for c in q_copies:
        c.wait_recv()

    row_tile = 128
    row_tiles = n_seq * rows_each // row_tile
    inverse = 1.0 / math.sqrt(head_dim)

    def attend(kv, scales, i, q):
        source = ((group + groups - i) % groups) * copies + (member + copies - q) % copies

        def one_tile(n, unused):
            at = pl.ds(pl.multiple_of(n * row_tile, row_tile), row_tile)
            queries = q_all[pl.ds(n * (row_tile // rows_each), row_tile // rows_each)].reshape(
                row_tile, head_dim
            )
            keys = kv[pl.ds(0, local_len), :]
            scores = lax.dot_general(
                queries, keys, (((1,), (1,)), ((), ())), preferred_element_type=jnp.float32
            )
            scores = scores * (scales[0:1, :] * inverse)
            key_pos = source * local_len + lax.broadcasted_iota(jnp.int32, (1, local_len), 1)
            row = n * row_tile + lax.broadcasted_iota(jnp.int32, (row_tile, 1), 0)
            query_pos = prefix_len + ((row // rows_each) * n_ep + zed) * tokens + row % tokens
            scores = jnp.where(key_pos <= query_pos, scores, hidden_score)
            old = top[at, :]
            new = jnp.maximum(old, jnp.max(scores, axis=1, keepdims=True))
            exp_scores = jnp.exp(scores - new[:, :1])
            shrink = jnp.exp(old - new)
            total[at, :] = total[at, :] * shrink + jnp.sum(exp_scores, axis=1, keepdims=True)
            weighted = (exp_scores * scales[1:2, :]).astype(jnp.bfloat16)
            acc[at, :] = acc[at, :] * shrink + jnp.dot(
                weighted, kv[pl.ds(local_len, local_len), :], preferred_element_type=jnp.float32
            )
            top[at, :] = new
            return unused

        lax.fori_loop(0, row_tiles, one_tile, 0)

    attend(kv_ref.at[group], scale_ref.at[group], 0, 0)
    for q in range(1, copies):
        for c in arrivals[0, q]:
            c.wait_recv()
        attend(kv_all.at[0, q], scale_all.at[0, q], 0, q)
    for i in range(1, groups):
        for c in arrivals[i, 0]:
            c.wait_recv()
        for q in range(1, copies):
            arrivals[i, q] = send_kv(
                kv_all.at[i, 0],
                scale_all.at[i, 0],
                i,
                q,
                group * copies + (member + q) % copies,
            )
        attend(kv_all.at[i, 0], scale_all.at[i, 0], i, 0)
    for i in range(1, groups):
        for q in range(1, copies):
            for c in arrivals[i, q]:
                c.wait_recv()
            attend(kv_all.at[i, q], scale_all.at[i, q], i, q)

    for src in range(n_seq):
        for h in range(heads):
            at = pl.ds(src * rows_each + h * tokens, tokens)
            wide[pl.ds(src * tokens, tokens), pl.ds(h * head_dim, head_dim)] = (
                acc[at, :] / total[at, :]
            )
    out_ref[...] = wide[...].astype(jnp.bfloat16)
    for c in q_copies:
        c.wait_send()
    for pair in pending:
        for c in pair:
            c.wait_send()


def layer_kernel(
    n_seq,
    n_ep,
    tokens,
    attn_ref,
    out_weight_ref,
    residual_ref,
    gain_ref,
    mix_ref,
    gate_ref,
    up_ref,
    down_ref,
    hidden_ref,
    expert_ref,
    attn_all,
    out_w,
    gate_w,
    up_w,
    down_w,
    part_out,
    part_in,
    col_out,
    col_in,
    mine,
    gathered,
    rows,
    gate_acc,
    up_acc,
    active,
    partial,
    pair_in,
    pair_sum,
    plane_in,
    tail_own,
    tail_out,
    tail_in,
    load_sem,
    local_sem,
    attn_send,
    attn_recv,
    part_send,
    part_recv,
    col_send,
    col_recv,
    a_send,
    a_recv,
    b_send,
    b_recv,
    c_send,
    c_recv,
    pair_send,
    pair_recv,
    plane_send,
    plane_recv,
    tail_send,
    tail_recv,
):
    me = lax.axis_index("seq")
    zed = lax.axis_index("ep")
    chips = n_seq // 2
    chip = me // 2
    core = me % 2
    other = chip * 2 + (1 - core)
    model = residual_ref.shape[1]
    half = model // 2
    bf16 = jnp.bfloat16
    f32 = jnp.float32

    loads = []
    for n, (src, dst) in enumerate(
        ((out_weight_ref, out_w), (gate_ref, gate_w), (up_ref, up_w), (down_ref, down_w))
    ):
        c = pltpu.make_async_copy(src, dst, load_sem.at[n])
        c.start()
        loads.append(c)

    barrier = pltpu.get_barrier_semaphore()
    for step in range(1, n_seq):
        pl.semaphore_signal(
            barrier, inc=1, device_id=device_at((me + step) % n_seq, zed), device_id_type=MESH
        )
    for step in range(1, n_ep):
        pl.semaphore_signal(
            barrier, inc=1, device_id=device_at(me, (zed + step) % n_ep), device_id_type=MESH
        )
    own = pltpu.make_async_copy(attn_ref, attn_all.at[zed], local_sem.at[0])
    own.start()
    pl.semaphore_wait(barrier, n_seq + n_ep - 2)

    sends = []

    def go(*args):
        c = remote(*args)
        c.start()
        sends.append(c)
        return c

    waits = [
        go(
            attn_ref,
            attn_all.at[zed],
            attn_send.at[j],
            attn_recv.at[j],
            me,
            (zed + j) % n_ep,
        )
        for j in range(1, n_ep)
    ]
    own.wait()
    loads[0].wait()
    for c in waits:
        c.wait_recv()

    cols = out_w.shape[1]
    depth = attn_ref.shape[1]
    part_waits = []
    attention = attn_all[...].reshape(n_ep * n_seq * tokens, depth)
    col_tile = 256
    for n in range(cols // col_tile):
        at = pl.ds(n * col_tile, col_tile)
        product = jnp.dot(attention, out_w[:, at], preferred_element_type=f32).reshape(
            n_ep, n_seq, tokens, col_tile
        )
        for s in range(n_seq):
            part_out[s, :, at] = product[:, s].reshape(n_ep * tokens, col_tile).astype(bf16)
    for step in range(1, n_seq):
        to = (me + step) % n_seq
        part_waits.append(
            go(
                part_out.at[to],
                part_in.at[step],
                part_send.at[step],
                part_recv.at[step],
                to,
                zed,
            )
        )
    for c in part_waits:
        c.wait_recv()
    summed = part_out[me].astype(f32)
    for step in range(1, n_seq):
        summed = summed + part_in[step].astype(f32)
    col_out[...] = summed.reshape(n_ep, tokens, cols)
    col_waits = []
    for j in range(1, n_ep):
        to = (zed + j) % n_ep
        col_waits.append(
            go(col_out.at[to], col_in.at[zed], col_send.at[j], col_recv.at[j], me, to)
        )
    keep = pltpu.make_async_copy(col_out.at[zed], col_in.at[zed], local_sem.at[1])
    keep.start()
    keep.wait()
    for c in col_waits:
        c.wait_recv()
    projected = jnp.concatenate([col_in[j] for j in range(n_ep)], axis=1)
    hidden = (residual_ref[...].astype(f32) + projected).astype(bf16)
    hidden_ref[...] = hidden
    wide = hidden.astype(f32)
    mean_square = jnp.mean(wide * wide, axis=1, keepdims=True)
    normed = wide * lax.rsqrt(mean_square + eps_norm) * gain_ref[...]
    mine[...] = jnp.concatenate([normed[:, :half], normed[:, half:]], axis=0).astype(bf16)

    keep = pltpu.make_async_copy(mine, gathered.at[core, chip, zed], local_sem.at[2])
    keep.start()
    spot = gathered.at[core, chip, zed]
    a_waits = {}
    b_waits = {}
    c_waits = []
    for j in range(1, n_ep):
        a_waits[j] = go(mine, spot, a_send.at[j], a_recv.at[j], me, (zed + j) % n_ep)

    def spread(src, at, j):
        for i in range(1, chips):
            to = ((chip + i) % chips) * 2 + core
            b_waits[i, j] = go(src, at, b_send.at[i, j], b_recv.at[i, j], to, zed)

    def across(src, at, i, j):
        c_waits.append(go(src, at, c_send.at[i, j], c_recv.at[i, j], other, zed))

    spread(mine, spot, 0)
    across(mine, spot, 0, 0)
    for j in range(1, n_ep):
        a_waits[j].wait_recv()
        at = gathered.at[core, chip, (zed + n_ep - j) % n_ep]
        spread(at, at, j)
        across(at, at, 0, j)
    for j in range(n_ep):
        for i in range(1, chips):
            b_waits[i, j].wait_recv()
            at = gathered.at[core, (chip + chips - i) % chips, (zed + n_ep - j) % n_ep]
            across(at, at, i, j)
    keep.wait()
    for c in c_waits:
        c.wait_recv()

    pairs = n_ep // 2

    def regroup(n, unused):
        blocks = gathered[n // (chips * pairs), (n // pairs) % chips, pl.ds((n % pairs) * 2, 2)]
        blocks = blocks.astype(f32)
        at = pl.ds(pl.multiple_of(n * 16, 16), 16)
        rows[at, pl.ds(0, half)] = jnp.concatenate(
            [blocks[0, :tokens], blocks[1, :tokens]], axis=0
        ).astype(bf16)
        rows[at, pl.ds(half, half)] = jnp.concatenate(
            [blocks[0, tokens:], blocks[1, tokens:]], axis=0
        ).astype(bf16)
        return unused

    lax.fori_loop(0, 2 * chips * pairs, regroup, 0)

    for c in loads[1:]:
        c.wait()
    gate_acc[...] = jnp.zeros_like(gate_acc)
    up_acc[...] = jnp.zeros_like(up_acc)
    depth_tile = 1024
    row_tile = 256
    count = rows.shape[0]

    def contract(n, unused):
        deep = pl.ds(pl.multiple_of(n * depth_tile, depth_tile), depth_tile)
        for r in range(count // row_tile):
            at = pl.ds(r * row_tile, row_tile)
            part = rows[at, deep]
            gate_acc[at, :] += jnp.dot(part, gate_w[deep, :], preferred_element_type=f32)
            up_acc[at, :] += jnp.dot(part, up_w[deep, :], preferred_element_type=f32)
        return unused

    lax.fori_loop(0, model // depth_tile, contract, 0)
    gate = gate_acc[...]
    active[...] = (gate / (1.0 + jnp.exp(-gate)) * up_acc[...]).astype(bf16)

    chunks = partial.shape[0]
    width = partial.shape[2]
    my_rows = count // 2
    chip_rows = n_ep * tokens
    pair_waits, plane_waits, tail_waits = {}, {}, {}

    def down(ch):
        deep = pl.ds(ch * width, width)
        for r in range(count // row_tile):
            at = pl.ds(r * row_tile, row_tile)
            for n in range(width // 256):
                deep = pl.ds(ch * width + n * 256, 256)
                y = jnp.dot(active[at, :], down_w[:, deep], preferred_element_type=f32)
                partial[ch, at, pl.ds(n * 256, 256)] = (y * mix_ref[at, :1]).astype(bf16)
        theirs = pl.ds(pl.multiple_of((1 - core) * my_rows, 16), my_rows)
        pair_waits[ch] = go(
            partial.at[ch, theirs],
            pair_in.at[ch],
            pair_send.at[ch],
            pair_recv.at[ch],
            other,
            zed,
        )

    def over_pair(ch):
        pair_waits[ch].wait_recv()
        ours = pl.ds(pl.multiple_of(core * my_rows, 16), my_rows)
        pair_sum[ch] = (partial[ch, ours, :].astype(f32) + pair_in[ch].astype(f32)).astype(bf16)
        for i in range(1, chips):
            goal = (chip + i) % chips
            plane_waits[ch, i] = go(
                pair_sum.at[ch, pl.ds(pl.multiple_of(goal * chip_rows, 16), chip_rows)],
                plane_in.at[ch, i],
                plane_send.at[ch, i],
                plane_recv.at[ch, i],
                goal * 2 + core,
                zed,
            )

    def over_plane(ch):
        for i in range(1, chips):
            plane_waits[ch, i].wait_recv()
        ours = pl.ds(pl.multiple_of(chip * chip_rows, 16), chip_rows)
        value = pair_sum[ch, ours, :].astype(f32)
        for i in range(1, chips):
            value = value + plane_in[ch, i].astype(f32)
        tail_own[ch] = value.reshape(n_ep, tokens, width)
        for j in range(n_ep):
            block = value[j * tokens : (j + 1) * tokens]
            tail_out[ch, j] = jnp.concatenate(
                [block[:, : width // 2], block[:, width // 2 :]], axis=0
            ).astype(bf16)
        for j in range(1, n_ep):
            to = (zed + j) % n_ep
            tail_waits[ch, j] = go(
                tail_out.at[ch, to],
                tail_in.at[ch, j],
                tail_send.at[ch, j],
                tail_recv.at[ch, j],
                me,
                to,
            )

    def finish(ch):
        value = tail_own[ch, zed]
        for j in range(1, n_ep):
            tail_waits[ch, j].wait_recv()
            got = tail_in[ch, j].astype(f32)
            value = value + jnp.concatenate([got[:tokens], got[tokens:]], axis=1)
        expert_ref[:, pl.ds(ch * width, width)] = value.astype(bf16)

    for step in range(chunks + 3):
        if step < chunks:
            down(step)
        if 0 <= step - 1 < chunks:
            over_pair(step - 1)
        if 0 <= step - 2 < chunks:
            over_plane(step - 2)
        if 0 <= step - 3 < chunks:
            finish(step - 3)
    for c in sends:
        c.wait_send()


def body(
    queries,
    key_codes,
    quantized_value_cache,
    key_scale,
    value_code_scale,
    out_weight,
    residual,
    norm_gain,
    route_ids,
    route_weight,
    w_gate,
    w_up,
    w_down,
):
    n_seq = lax.axis_size("seq")
    n_ep = lax.axis_size("ep")
    tokens, heads_all, head_dim = queries.shape
    local_len, kv_heads = key_scale.shape
    window_len = tokens * n_seq * n_ep
    prefix_len = local_len * n_seq - window_len
    heads = heads_all // n_seq
    copies = n_seq // kv_heads
    groups = n_seq // copies
    bf16, f32 = jnp.bfloat16, jnp.float32
    model = residual.shape[1]
    experts = n_seq * n_ep // 2

    mix = route_weight / jnp.sum(route_weight, axis=1, keepdims=True)
    grid = jnp.arange(experts, dtype=jnp.int32)
    dense = jnp.sum(
        jnp.where(route_ids[:, :, None] == grid[None, None, :], mix[:, :, None], 0.0), axis=1
    )
    everyone = lax.all_gather(dense, ("seq", "ep"), axis=0, tiled=True)
    expert = (lax.axis_index("seq") * n_ep + lax.axis_index("ep")) // 2
    my_mix = jnp.sum(jnp.where(grid[None, :] == expert, everyone, 0.0), axis=1)
    my_mix = my_mix.reshape(n_seq // 2, 2, n_ep * tokens).transpose(1, 0, 2)
    my_mix = jnp.broadcast_to(my_mix.reshape(window_len, 1), (window_len, 128))

    q_sorted = (
        queries.reshape(tokens, n_seq, heads, head_dim)
        .transpose(1, 2, 0, 3)
        .reshape(n_seq, heads * tokens, head_dim)
    )
    kv = jnp.concatenate(
        [key_codes.transpose(1, 0, 2), quantized_value_cache.transpose(1, 0, 2)], axis=1
    )
    scales = jnp.stack([key_scale.T, value_code_scale.T], axis=1).astype(f32)
    scales = jnp.pad(scales, ((0, 0), (0, 6), (0, 0)))
    q_rows = n_seq * heads * tokens
    vmem = pl.BlockSpec(memory_space=pltpu.VMEM)
    hbm = pl.BlockSpec(memory_space=pl.ANY)
    dma = pltpu.SemaphoreType.DMA
    attention = pl.pallas_call(
        functools.partial(attention_kernel, n_seq, n_ep, copies, tokens, heads, prefix_len),
        out_shape=jax.ShapeDtypeStruct((n_seq * tokens, heads * head_dim), bf16),
        in_specs=[vmem] * 3,
        out_specs=vmem,
        scratch_shapes=[
            pltpu.VMEM((n_seq, heads * tokens, head_dim), bf16),
            pltpu.VMEM((groups, copies, 2 * local_len, head_dim), bf16),
            pltpu.VMEM((groups, copies, 8, local_len), f32),
            pltpu.VMEM((q_rows, head_dim), f32),
            pltpu.VMEM((q_rows, head_dim), f32),
            pltpu.VMEM((q_rows, head_dim), f32),
            pltpu.VMEM((n_seq * tokens, heads * head_dim), f32),
            dma((n_seq,)),
            dma((n_seq,)),
            dma((groups, copies)),
            dma((groups, copies)),
            dma((groups, copies)),
            dma((groups, copies)),
            dma,
        ],
        compiler_params=pltpu.CompilerParams(
            collective_id=0, has_side_effects=True, vmem_limit_bytes=40 << 20
        ),
        name="attention",
    )(q_sorted, kv, scales)

    cols = out_weight.shape[1]
    depth = out_weight.shape[0]
    wide = w_gate.shape[1]
    chips = n_seq // 2
    chunks = 4
    width = model // chunks
    return pl.pallas_call(
        functools.partial(layer_kernel, n_seq, n_ep, tokens),
        out_shape=(
            jax.ShapeDtypeStruct((tokens, model), bf16),
            jax.ShapeDtypeStruct((tokens, model), bf16),
        ),
        in_specs=[vmem, hbm, vmem, vmem, vmem, hbm, hbm, hbm],
        out_specs=(vmem, vmem),
        scratch_shapes=[
            pltpu.VMEM((n_ep, n_seq * tokens, depth), bf16),
            pltpu.VMEM((depth, cols), bf16),
            pltpu.VMEM((model, wide), bf16),
            pltpu.VMEM((model, wide), bf16),
            pltpu.VMEM((wide, model), bf16),
            pltpu.VMEM((n_seq, n_ep * tokens, cols), bf16),
            pltpu.VMEM((n_seq, n_ep * tokens, cols), bf16),
            pltpu.VMEM((n_ep, tokens, cols), f32),
            pltpu.VMEM((n_ep, tokens, cols), f32),
            pltpu.VMEM((2 * tokens, model // 2), bf16),
            pltpu.VMEM((2, chips, n_ep, 2 * tokens, model // 2), bf16),
            pltpu.VMEM((window_len, model), bf16),
            pltpu.VMEM((window_len, wide), f32),
            pltpu.VMEM((window_len, wide), f32),
            pltpu.VMEM((window_len, wide), bf16),
            pltpu.VMEM((chunks, window_len, width), bf16),
            pltpu.VMEM((chunks, window_len // 2, width), bf16),
            pltpu.VMEM((chunks, window_len // 2, width), bf16),
            pltpu.VMEM((chunks, chips, n_ep * tokens, width), bf16),
            pltpu.VMEM((chunks, n_ep, tokens, width), f32),
            pltpu.VMEM((chunks, n_ep, 2 * tokens, width // 2), bf16),
            pltpu.VMEM((chunks, n_ep, 2 * tokens, width // 2), bf16),
            dma((4,)),
            dma((3,)),
            dma((n_ep,)),
            dma((n_ep,)),
            dma((n_seq,)),
            dma((n_seq,)),
            dma((n_ep,)),
            dma((n_ep,)),
            dma((n_ep,)),
            dma((n_ep,)),
            dma((chips, n_ep)),
            dma((chips, n_ep)),
            dma((chips, n_ep)),
            dma((chips, n_ep)),
            dma((chunks,)),
            dma((chunks,)),
            dma((chunks, chips)),
            dma((chunks, chips)),
            dma((chunks, n_ep)),
            dma((chunks, n_ep)),
        ],
        compiler_params=pltpu.CompilerParams(
            collective_id=1, has_side_effects=True, vmem_limit_bytes=60 << 20
        ),
        name="layer",
    )(
        attention,
        out_weight,
        residual,
        norm_gain.reshape(1, model),
        my_mix,
        w_gate,
        w_up,
        w_down,
    )


def solution(mesh):
    placed = (
        P(("grp", "seq", "ep"), None, None),
        P(("grp", "seq"), None, None),
        P(("grp", "seq"), None, None),
        P(("grp", "seq"), None),
        P(("grp", "seq"), None),
        P("seq", "ep"),
        P(("grp", "seq", "ep"), None),
        P(),
        P(("grp", "seq", "ep"), None),
        P(("grp", "seq", "ep"), None),
        P(None, ("seq", "ep")),
        P(None, ("seq", "ep")),
        P(("seq", "ep"), None),
    )
    return jax.shard_map(
        body,
        mesh=mesh,
        in_specs=placed,
        out_specs=(P(("grp", "seq", "ep"), None), P(("grp", "seq", "ep"), None)),
        check_vma=False,
    )
```

```python
import functools
import math

import jax
import jax.numpy as jnp
from jax import lax
from jax.experimental import pallas as pl
from jax.experimental.pallas import tpu as pltpu
from jax.sharding import PartitionSpec as P

eps_norm = 1e-06
MESH = pl.DeviceIdType.MESH
hidden_score = -1e30


def device_at(seq_pos, ep_pos):
    return {"seq": seq_pos, "ep": ep_pos}


def remote(src, dst, send_sem, recv_sem, seq_pos, ep_pos):
    return pltpu.make_async_remote_copy(
        src_ref=src,
        dst_ref=dst,
        send_sem=send_sem,
        recv_sem=recv_sem,
        device_id=device_at(seq_pos, ep_pos),
        device_id_type=MESH,
    )


def attention_kernel(
    n_seq,
    n_ep,
    copies,
    tokens,
    heads,
    prefix_len,
    q_ref,
    kv_ref,
    scale_ref,
    out_ref,
    q_all,
    kv_all,
    scale_all,
    top,
    total,
    acc,
    wide,
    q_send,
    q_recv,
    kv_send,
    kv_recv,
    scale_send,
    scale_recv,
    own_sem,
):
    me = lax.axis_index("seq")
    zed = lax.axis_index("ep")
    groups = n_seq // copies
    group = me // copies
    member = me % copies
    head_dim = q_ref.shape[2]
    local_len = scale_ref.shape[2]
    rows_each = tokens * heads

    barrier = pltpu.get_barrier_semaphore()
    for step in range(1, n_seq):
        pl.semaphore_signal(
            barrier,
            inc=1,
            device_id=device_at((me + step) % n_seq, zed),
            device_id_type=MESH,
        )
    own = pltpu.make_async_copy(q_ref.at[me], q_all.at[me], own_sem)
    own.start()
    top[...] = jnp.full_like(top, hidden_score)
    total[...] = jnp.zeros_like(total)
    acc[...] = jnp.zeros_like(acc)
    pl.semaphore_wait(barrier, n_seq - 1)

    pending = []
    q_copies = []
    for step in range(1, n_seq):
        to = (me + step) % n_seq
        c = remote(q_ref.at[to], q_all.at[me], q_send.at[step], q_recv.at[step], to, zed)
        c.start()
        q_copies.append(c)

    def send_kv(kv_src, scale_src, i, q, to):
        a = remote(kv_src, kv_all.at[i, q], kv_send.at[i, q], kv_recv.at[i, q], to, zed)
        b = remote(
            scale_src, scale_all.at[i, q], scale_send.at[i, q], scale_recv.at[i, q], to, zed
        )
        a.start()
        b.start()
        pending.append((a, b))
        return (a, b)

    arrivals = {}
    for i in range(1, groups):
        goal = (group + i) % groups
        arrivals[i, 0] = send_kv(
            kv_ref.at[goal], scale_ref.at[goal], i, 0, goal * copies + member
        )
    for q in range(1, copies):
        arrivals[0, q] = send_kv(
            kv_ref.at[group],
            scale_ref.at[group],
            0,
            q,
            group * copies + (member + q) % copies,
        )

    own.wait()
    for c in q_copies:
        c.wait_recv()

    row_tile = 256
    row_tiles = n_seq * rows_each // row_tile
    inverse = 1.0 / math.sqrt(head_dim)

    def attend(kv, scales, i, q):
        source = ((group + groups - i) % groups) * copies + (member + copies - q) % copies

        def one_tile(n, unused):
            at = pl.ds(pl.multiple_of(n * row_tile, row_tile), row_tile)
            queries = q_all[pl.ds(n * (row_tile // rows_each), row_tile // rows_each)].reshape(
                row_tile, head_dim
            )
            keys = kv[pl.ds(0, local_len), :]
            scores = lax.dot_general(
                queries, keys, (((1,), (1,)), ((), ())), preferred_element_type=jnp.float32
            )
            scores = scores * (scales[0:1, :] * inverse)
            key_pos = source * local_len + lax.broadcasted_iota(jnp.int32, (1, local_len), 1)
            row = n * row_tile + lax.broadcasted_iota(jnp.int32, (row_tile, 1), 0)
            query_pos = prefix_len + ((row // rows_each) * n_ep + zed) * tokens + row % tokens
            scores = jnp.where(key_pos <= query_pos, scores, hidden_score)
            old = top[at, :]
            new = jnp.maximum(old, jnp.max(scores, axis=1, keepdims=True))
            exp_scores = jnp.exp(scores - new[:, :1])
            shrink = jnp.exp(old - new)
            total[at, :] = total[at, :] * shrink + jnp.sum(exp_scores, axis=1, keepdims=True)
            weighted = (exp_scores * scales[1:2, :]).astype(jnp.bfloat16)
            acc[at, :] = acc[at, :] * shrink + jnp.dot(
                weighted, kv[pl.ds(local_len, local_len), :], preferred_element_type=jnp.float32
            )
            top[at, :] = new
            return unused

        lax.fori_loop(0, row_tiles, one_tile, 0)

    attend(kv_ref.at[group], scale_ref.at[group], 0, 0)
    for q in range(1, copies):
        for c in arrivals[0, q]:
            c.wait_recv()
        attend(kv_all.at[0, q], scale_all.at[0, q], 0, q)
    for i in range(1, groups):
        for c in arrivals[i, 0]:
            c.wait_recv()
        for q in range(1, copies):
            arrivals[i, q] = send_kv(
                kv_all.at[i, 0],
                scale_all.at[i, 0],
                i,
                q,
                group * copies + (member + q) % copies,
            )
        attend(kv_all.at[i, 0], scale_all.at[i, 0], i, 0)
    for i in range(1, groups):
        for q in range(1, copies):
            for c in arrivals[i, q]:
                c.wait_recv()
            attend(kv_all.at[i, q], scale_all.at[i, q], i, q)

    for src in range(n_seq):
        for h in range(heads):
            at = pl.ds(src * rows_each + h * tokens, tokens)
            wide[pl.ds(src * tokens, tokens), pl.ds(h * head_dim, head_dim)] = (
                acc[at, :] / total[at, :]
            )
    out_ref[...] = wide[...].astype(jnp.bfloat16)
    for c in q_copies:
        c.wait_send()
    for pair in pending:
        for c in pair:
            c.wait_send()


def layer_kernel(
    n_seq,
    n_ep,
    tokens,
    attn_ref,
    out_weight_ref,
    residual_ref,
    gain_ref,
    mix_ref,
    gate_ref,
    up_ref,
    down_ref,
    hidden_ref,
    expert_ref,
    attn_all,
    mix_line,
    mix_all,
    mix_rows,
    out_w,
    gate_w,
    up_w,
    down_w,
    part_out,
    part_in,
    col_out,
    col_in,
    mine,
    gathered,
    rows,
    gate_acc,
    up_acc,
    active,
    partial,
    pair_in,
    pair_sum,
    plane_in,
    tail_own,
    tail_out,
    tail_in,
    load_sem,
    local_sem,
    line_send,
    line_recv,
    mix_send,
    mix_recv,
    attn_send,
    attn_recv,
    part_send,
    part_recv,
    col_send,
    col_recv,
    a_send,
    a_recv,
    b_send,
    b_recv,
    c_send,
    c_recv,
    pair_send,
    pair_recv,
    plane_send,
    plane_recv,
    tail_send,
    tail_recv,
):
    me = lax.axis_index("seq")
    zed = lax.axis_index("ep")
    chips = n_seq // 2
    chip = me // 2
    core = me % 2
    other = chip * 2 + (1 - core)
    model = residual_ref.shape[1]
    half = model // 2
    bf16 = jnp.bfloat16
    f32 = jnp.float32

    loads = []
    for n, (src, dst) in enumerate(
        ((out_weight_ref, out_w), (gate_ref, gate_w), (up_ref, up_w), (down_ref, down_w))
    ):
        c = pltpu.make_async_copy(src, dst, load_sem.at[n])
        c.start()
        loads.append(c)

    barrier = pltpu.get_barrier_semaphore()
    for step in range(1, n_seq):
        pl.semaphore_signal(
            barrier, inc=1, device_id=device_at((me + step) % n_seq, zed), device_id_type=MESH
        )
    for step in range(1, n_ep):
        pl.semaphore_signal(
            barrier, inc=1, device_id=device_at(me, (zed + step) % n_ep), device_id_type=MESH
        )
    own = pltpu.make_async_copy(attn_ref, attn_all.at[zed], local_sem.at[0])
    own.start()
    pl.semaphore_wait(barrier, n_seq + n_ep - 2)

    sends = []

    def go(*args):
        c = remote(*args)
        c.start()
        sends.append(c)
        return c

    waits = [
        go(
            attn_ref,
            attn_all.at[zed],
            attn_send.at[j],
            attn_recv.at[j],
            me,
            (zed + j) % n_ep,
        )
        for j in range(1, n_ep)
    ]
    line_keep = pltpu.make_async_copy(mix_ref, mix_line.at[zed], local_sem.at[3])
    line_keep.start()
    line_waits = [
        go(
            mix_ref,
            mix_line.at[zed],
            line_send.at[j],
            line_recv.at[j],
            me,
            (zed + j) % n_ep,
        )
        for j in range(1, n_ep)
    ]
    own.wait()
    loads[0].wait()
    for c in waits:
        c.wait_recv()

    cols = out_w.shape[1]
    depth = attn_ref.shape[1]
    part_waits = []
    attention = attn_all[...].reshape(n_ep * n_seq * tokens, depth)
    col_tile = 256
    for n in range(cols // col_tile):
        at = pl.ds(n * col_tile, col_tile)
        product = jnp.dot(attention, out_w[:, at], preferred_element_type=f32).reshape(
            n_ep, n_seq, tokens, col_tile
        )
        for s in range(n_seq):
            part_out[s, :, at] = product[:, s].reshape(n_ep * tokens, col_tile).astype(bf16)
    for step in range(1, n_seq):
        to = (me + step) % n_seq
        part_waits.append(
            go(
                part_out.at[to],
                part_in.at[step],
                part_send.at[step],
                part_recv.at[step],
                to,
                zed,
            )
        )
    line_keep.wait()
    for c in line_waits:
        c.wait_recv()
    mix_keep = pltpu.make_async_copy(mix_line, mix_all.at[me], local_sem.at[4])
    mix_keep.start()
    mix_waits = [
        go(
            mix_line,
            mix_all.at[me],
            mix_send.at[step],
            mix_recv.at[step],
            (me + step) % n_seq,
            zed,
        )
        for step in range(1, n_seq)
    ]
    for c in part_waits:
        c.wait_recv()
    summed = part_out[me].astype(f32)
    for step in range(1, n_seq):
        summed = summed + part_in[step].astype(f32)
    col_out[...] = summed.reshape(n_ep, tokens, cols)
    col_waits = []
    for j in range(1, n_ep):
        to = (zed + j) % n_ep
        col_waits.append(
            go(col_out.at[to], col_in.at[zed], col_send.at[j], col_recv.at[j], me, to)
        )
    keep = pltpu.make_async_copy(col_out.at[zed], col_in.at[zed], local_sem.at[1])
    keep.start()
    keep.wait()
    for c in col_waits:
        c.wait_recv()
    projected = jnp.concatenate([col_in[j] for j in range(n_ep)], axis=1)
    hidden = (residual_ref[...].astype(f32) + projected).astype(bf16)
    hidden_ref[...] = hidden
    wide = hidden.astype(f32)
    mean_square = jnp.mean(wide * wide, axis=1, keepdims=True)
    normed = wide * lax.rsqrt(mean_square + eps_norm) * gain_ref[...]
    mine[...] = jnp.concatenate([normed[:, :half], normed[:, half:]], axis=0).astype(bf16)

    keep = pltpu.make_async_copy(mine, gathered.at[core, chip, zed], local_sem.at[2])
    keep.start()
    spot = gathered.at[core, chip, zed]
    a_waits = {}
    b_waits = {}
    c_waits = []
    for j in range(1, n_ep):
        a_waits[j] = go(mine, spot, a_send.at[j], a_recv.at[j], me, (zed + j) % n_ep)

    def spread(src, at, j):
        for i in range(1, chips):
            to = ((chip + i) % chips) * 2 + core
            b_waits[i, j] = go(src, at, b_send.at[i, j], b_recv.at[i, j], to, zed)

    def across(src, at, i, j):
        c_waits.append(go(src, at, c_send.at[i, j], c_recv.at[i, j], other, zed))

    spread(mine, spot, 0)
    across(mine, spot, 0, 0)
    for j in range(1, n_ep):
        a_waits[j].wait_recv()
        at = gathered.at[core, chip, (zed + n_ep - j) % n_ep]
        spread(at, at, j)
        across(at, at, 0, j)
    mix_keep.wait()
    for c in mix_waits:
        c.wait_recv()
    expert = (me * n_ep + zed) // 2
    lane = lax.broadcasted_iota(jnp.int32, (1, mix_ref.shape[1]), 1)
    group_rows = n_ep * tokens
    for s in range(n_seq):
        weights = mix_all[s].reshape(group_rows, mix_ref.shape[1])
        weights = jnp.sum(jnp.where(lane == expert, weights, 0.0), axis=1, keepdims=True)
        at = pl.ds(((s % 2) * chips + s // 2) * group_rows, group_rows)
        mix_rows[at, :] = jnp.broadcast_to(weights, (group_rows, 128))
    for j in range(n_ep):
        for i in range(1, chips):
            b_waits[i, j].wait_recv()
            at = gathered.at[core, (chip + chips - i) % chips, (zed + n_ep - j) % n_ep]
            across(at, at, i, j)
    keep.wait()
    for c in c_waits:
        c.wait_recv()

    pairs = n_ep // 2

    def regroup(n, unused):
        blocks = gathered[n // (chips * pairs), (n // pairs) % chips, pl.ds((n % pairs) * 2, 2)]
        blocks = blocks.astype(f32)
        at = pl.ds(pl.multiple_of(n * 16, 16), 16)
        rows[at, pl.ds(0, half)] = jnp.concatenate(
            [blocks[0, :tokens], blocks[1, :tokens]], axis=0
        ).astype(bf16)
        rows[at, pl.ds(half, half)] = jnp.concatenate(
            [blocks[0, tokens:], blocks[1, tokens:]], axis=0
        ).astype(bf16)
        return unused

    lax.fori_loop(0, 2 * chips * pairs, regroup, 0)

    for c in loads[1:]:
        c.wait()
    gate_acc[...] = jnp.zeros_like(gate_acc)
    up_acc[...] = jnp.zeros_like(up_acc)
    depth_tile = 1024
    row_tile = 256
    count = rows.shape[0]

    def contract(n, unused):
        deep = pl.ds(pl.multiple_of(n * depth_tile, depth_tile), depth_tile)
        for r in range(count // row_tile):
            at = pl.ds(r * row_tile, row_tile)
            part = rows[at, deep]
            gate_acc[at, :] += jnp.dot(part, gate_w[deep, :], preferred_element_type=f32)
            up_acc[at, :] += jnp.dot(part, up_w[deep, :], preferred_element_type=f32)
        return unused

    lax.fori_loop(0, model // depth_tile, contract, 0)
    gate = gate_acc[...]
    active[...] = (gate / (1.0 + jnp.exp(-gate)) * up_acc[...]).astype(bf16)

    chunks = partial.shape[0]
    width = partial.shape[2]
    my_rows = count // 2
    chip_rows = n_ep * tokens
    pair_waits, plane_waits, tail_waits = {}, {}, {}

    def down(ch):
        deep = pl.ds(ch * width, width)
        for r in range(count // row_tile):
            at = pl.ds(r * row_tile, row_tile)
            for n in range(width // 256):
                deep = pl.ds(ch * width + n * 256, 256)
                y = jnp.dot(active[at, :], down_w[:, deep], preferred_element_type=f32)
                partial[ch, at, pl.ds(n * 256, 256)] = (y * mix_rows[at, :1]).astype(bf16)
        theirs = pl.ds(pl.multiple_of((1 - core) * my_rows, 16), my_rows)
        pair_waits[ch] = go(
            partial.at[ch, theirs],
            pair_in.at[ch],
            pair_send.at[ch],
            pair_recv.at[ch],
            other,
            zed,
        )

    def over_pair(ch):
        pair_waits[ch].wait_recv()
        ours = pl.ds(pl.multiple_of(core * my_rows, 16), my_rows)
        pair_sum[ch] = (partial[ch, ours, :].astype(f32) + pair_in[ch].astype(f32)).astype(bf16)
        for i in range(1, chips):
            goal = (chip + i) % chips
            plane_waits[ch, i] = go(
                pair_sum.at[ch, pl.ds(pl.multiple_of(goal * chip_rows, 16), chip_rows)],
                plane_in.at[ch, i],
                plane_send.at[ch, i],
                plane_recv.at[ch, i],
                goal * 2 + core,
                zed,
            )

    def over_plane(ch):
        for i in range(1, chips):
            plane_waits[ch, i].wait_recv()
        ours = pl.ds(pl.multiple_of(chip * chip_rows, 16), chip_rows)
        value = pair_sum[ch, ours, :].astype(f32)
        for i in range(1, chips):
            value = value + plane_in[ch, i].astype(f32)
        tail_own[ch] = value.reshape(n_ep, tokens, width)
        for j in range(n_ep):
            block = value[j * tokens : (j + 1) * tokens]
            tail_out[ch, j] = jnp.concatenate(
                [block[:, : width // 2], block[:, width // 2 :]], axis=0
            ).astype(bf16)
        for j in range(1, n_ep):
            to = (zed + j) % n_ep
            tail_waits[ch, j] = go(
                tail_out.at[ch, to],
                tail_in.at[ch, j],
                tail_send.at[ch, j],
                tail_recv.at[ch, j],
                me,
                to,
            )

    def finish(ch):
        value = tail_own[ch, zed]
        for j in range(1, n_ep):
            tail_waits[ch, j].wait_recv()
            got = tail_in[ch, j].astype(f32)
            value = value + jnp.concatenate([got[:tokens], got[tokens:]], axis=1)
        expert_ref[:, pl.ds(ch * width, width)] = value.astype(bf16)

    for step in range(chunks + 3):
        if step < chunks:
            down(step)
        if 0 <= step - 1 < chunks:
            over_pair(step - 1)
        if 0 <= step - 2 < chunks:
            over_plane(step - 2)
        if 0 <= step - 3 < chunks:
            finish(step - 3)
    for c in sends:
        c.wait_send()


def body(
    queries,
    key_codes,
    quantized_value_cache,
    key_scale,
    value_code_scale,
    out_weight,
    residual,
    norm_gain,
    route_ids,
    route_weight,
    w_gate,
    w_up,
    w_down,
):
    n_seq = lax.axis_size("seq")
    n_ep = lax.axis_size("ep")
    tokens, heads_all, head_dim = queries.shape
    local_len, kv_heads = key_scale.shape
    window_len = tokens * n_seq * n_ep
    prefix_len = local_len * n_seq - window_len
    heads = heads_all // n_seq
    copies = n_seq // kv_heads
    groups = n_seq // copies
    bf16, f32 = jnp.bfloat16, jnp.float32
    model = residual.shape[1]
    experts = n_seq * n_ep // 2

    mix = route_weight / jnp.sum(route_weight, axis=1, keepdims=True)
    grid = jnp.arange(experts, dtype=jnp.int32)
    dense = jnp.sum(
        jnp.where(route_ids[:, :, None] == grid[None, None, :], mix[:, :, None], 0.0), axis=1
    )
    lanes = -(-experts // 128) * 128
    dense = jnp.pad(dense, ((0, 0), (0, lanes - experts)))

    q_sorted = (
        queries.reshape(tokens, n_seq, heads, head_dim)
        .transpose(1, 2, 0, 3)
        .reshape(n_seq, heads * tokens, head_dim)
    )
    kv = jnp.concatenate(
        [key_codes.transpose(1, 0, 2), quantized_value_cache.transpose(1, 0, 2)], axis=1
    )
    scales = jnp.stack([key_scale.T, value_code_scale.T], axis=1).astype(f32)
    scales = jnp.pad(scales, ((0, 0), (0, 6), (0, 0)))
    q_rows = n_seq * heads * tokens
    vmem = pl.BlockSpec(memory_space=pltpu.VMEM)
    hbm = pl.BlockSpec(memory_space=pl.ANY)
    dma = pltpu.SemaphoreType.DMA
    attention = pl.pallas_call(
        functools.partial(attention_kernel, n_seq, n_ep, copies, tokens, heads, prefix_len),
        out_shape=jax.ShapeDtypeStruct((n_seq * tokens, heads * head_dim), bf16),
        in_specs=[vmem] * 3,
        out_specs=vmem,
        scratch_shapes=[
            pltpu.VMEM((n_seq, heads * tokens, head_dim), bf16),
            pltpu.VMEM((groups, copies, 2 * local_len, head_dim), bf16),
            pltpu.VMEM((groups, copies, 8, local_len), f32),
            pltpu.VMEM((q_rows, head_dim), f32),
            pltpu.VMEM((q_rows, head_dim), f32),
            pltpu.VMEM((q_rows, head_dim), f32),
            pltpu.VMEM((n_seq * tokens, heads * head_dim), f32),
            dma((n_seq,)),
            dma((n_seq,)),
            dma((groups, copies)),
            dma((groups, copies)),
            dma((groups, copies)),
            dma((groups, copies)),
            dma,
        ],
        compiler_params=pltpu.CompilerParams(
            collective_id=0, has_side_effects=True, vmem_limit_bytes=40 << 20
        ),
        name="attention",
    )(q_sorted, kv, scales)

    cols = out_weight.shape[1]
    depth = out_weight.shape[0]
    wide = w_gate.shape[1]
    chips = n_seq // 2
    chunks = 4
    width = model // chunks
    return pl.pallas_call(
        functools.partial(layer_kernel, n_seq, n_ep, tokens),
        out_shape=(
            jax.ShapeDtypeStruct((tokens, model), bf16),
            jax.ShapeDtypeStruct((tokens, model), bf16),
        ),
        in_specs=[vmem, hbm, vmem, vmem, vmem, hbm, hbm, hbm],
        out_specs=(vmem, vmem),
        scratch_shapes=[
            pltpu.VMEM((n_ep, n_seq * tokens, depth), bf16),
            pltpu.VMEM((n_ep, tokens, lanes), f32),
            pltpu.VMEM((n_seq, n_ep, tokens, lanes), f32),
            pltpu.VMEM((window_len, 128), f32),
            pltpu.VMEM((depth, cols), bf16),
            pltpu.VMEM((model, wide), bf16),
            pltpu.VMEM((model, wide), bf16),
            pltpu.VMEM((wide, model), bf16),
            pltpu.VMEM((n_seq, n_ep * tokens, cols), bf16),
            pltpu.VMEM((n_seq, n_ep * tokens, cols), bf16),
            pltpu.VMEM((n_ep, tokens, cols), f32),
            pltpu.VMEM((n_ep, tokens, cols), f32),
            pltpu.VMEM((2 * tokens, model // 2), bf16),
            pltpu.VMEM((2, chips, n_ep, 2 * tokens, model // 2), bf16),
            pltpu.VMEM((window_len, model), bf16),
            pltpu.VMEM((window_len, wide), f32),
            pltpu.VMEM((window_len, wide), f32),
            pltpu.VMEM((window_len, wide), bf16),
            pltpu.VMEM((chunks, window_len, width), bf16),
            pltpu.VMEM((chunks, window_len // 2, width), bf16),
            pltpu.VMEM((chunks, window_len // 2, width), bf16),
            pltpu.VMEM((chunks, chips, n_ep * tokens, width), bf16),
            pltpu.VMEM((chunks, n_ep, tokens, width), f32),
            pltpu.VMEM((chunks, n_ep, 2 * tokens, width // 2), bf16),
            pltpu.VMEM((chunks, n_ep, 2 * tokens, width // 2), bf16),
            dma((4,)),
            dma((5,)),
            dma((n_ep,)),
            dma((n_ep,)),
            dma((n_seq,)),
            dma((n_seq,)),
            dma((n_ep,)),
            dma((n_ep,)),
            dma((n_seq,)),
            dma((n_seq,)),
            dma((n_ep,)),
            dma((n_ep,)),
            dma((n_ep,)),
            dma((n_ep,)),
            dma((chips, n_ep)),
            dma((chips, n_ep)),
            dma((chips, n_ep)),
            dma((chips, n_ep)),
            dma((chunks,)),
            dma((chunks,)),
            dma((chunks, chips)),
            dma((chunks, chips)),
            dma((chunks, n_ep)),
            dma((chunks, n_ep)),
        ],
        compiler_params=pltpu.CompilerParams(
            collective_id=1, has_side_effects=True, vmem_limit_bytes=60 << 20
        ),
        name="layer",
    )(
        attention,
        out_weight,
        residual,
        norm_gain.reshape(1, model),
        dense,
        w_gate,
        w_up,
        w_down,
    )


def solution(mesh):
    placed = (
        P(("grp", "seq", "ep"), None, None),
        P(("grp", "seq"), None, None),
        P(("grp", "seq"), None, None),
        P(("grp", "seq"), None),
        P(("grp", "seq"), None),
        P("seq", "ep"),
        P(("grp", "seq", "ep"), None),
        P(),
        P(("grp", "seq", "ep"), None),
        P(("grp", "seq", "ep"), None),
        P(None, ("seq", "ep")),
        P(None, ("seq", "ep")),
        P(("seq", "ep"), None),
    )
    return jax.shard_map(
        body,
        mesh=mesh,
        in_specs=placed,
        out_specs=(P(("grp", "seq", "ep"), None), P(("grp", "seq", "ep"), None)),
        check_vma=False,
    )
```

```python
import functools
import math

import jax
import jax.numpy as jnp
from jax import lax
from jax.experimental import pallas as pl
from jax.experimental.pallas import tpu as pltpu
from jax.sharding import PartitionSpec as P

eps_norm = 1e-06
MESH = pl.DeviceIdType.MESH
hidden_score = -1e30


def device_at(seq_pos, ep_pos):
    return {"seq": seq_pos, "ep": ep_pos}


def remote(src, dst, send_sem, recv_sem, seq_pos, ep_pos):
    return pltpu.make_async_remote_copy(
        src_ref=src,
        dst_ref=dst,
        send_sem=send_sem,
        recv_sem=recv_sem,
        device_id=device_at(seq_pos, ep_pos),
        device_id_type=MESH,
    )


def attention_part(
    go,
    n_seq,
    n_ep,
    copies,
    tokens,
    heads,
    prefix_len,
    q_ref,
    kv_ref,
    scale_ref,
    q_all,
    kv_all,
    scale_all,
    top,
    total,
    acc,
    wide,
    q_send,
    q_recv,
    kv_send,
    kv_recv,
    scale_send,
    scale_recv,
    own_sem,
    attn_all,
    attn_send,
    attn_recv,
):
    me = lax.axis_index("seq")
    zed = lax.axis_index("ep")
    groups = n_seq // copies
    group = me // copies
    member = me % copies
    head_dim = q_ref.shape[2]
    local_len = scale_ref.shape[2]
    rows_each = tokens * heads

    own = pltpu.make_async_copy(q_ref.at[me], q_all.at[me], own_sem)
    own.start()
    top[...] = jnp.full_like(top, hidden_score)
    total[...] = jnp.zeros_like(total)
    acc[...] = jnp.zeros_like(acc)
    pl.semaphore_wait(pltpu.get_barrier_semaphore(), n_seq + n_ep - 2)

    pending = []
    q_copies = []
    for step in range(1, n_seq):
        to = (me + step) % n_seq
        c = remote(q_ref.at[to], q_all.at[me], q_send.at[step], q_recv.at[step], to, zed)
        c.start()
        q_copies.append(c)

    def send_kv(kv_src, scale_src, i, q, to):
        a = remote(kv_src, kv_all.at[i, q], kv_send.at[i, q], kv_recv.at[i, q], to, zed)
        b = remote(
            scale_src, scale_all.at[i, q], scale_send.at[i, q], scale_recv.at[i, q], to, zed
        )
        a.start()
        b.start()
        pending.append((a, b))
        return (a, b)

    arrivals = {}
    for i in range(1, groups):
        goal = (group + i) % groups
        arrivals[i, 0] = send_kv(
            kv_ref.at[goal], scale_ref.at[goal], i, 0, goal * copies + member
        )
    for q in range(1, copies):
        arrivals[0, q] = send_kv(
            kv_ref.at[group],
            scale_ref.at[group],
            0,
            q,
            group * copies + (member + q) % copies,
        )

    own.wait()
    for c in q_copies:
        c.wait_recv()

    row_tile = 256
    row_tiles = n_seq * rows_each // row_tile
    inverse = 1.0 / math.sqrt(head_dim)

    def attend(kv, scales, i, q, first=0, last=row_tiles):
        source = ((group + groups - i) % groups) * copies + (member + copies - q) % copies

        def one_tile(n, unused):
            at = pl.ds(pl.multiple_of(n * row_tile, row_tile), row_tile)
            queries = q_all[pl.ds(n * (row_tile // rows_each), row_tile // rows_each)].reshape(
                row_tile, head_dim
            )
            keys = kv[pl.ds(0, local_len), :]
            scores = lax.dot_general(
                queries, keys, (((1,), (1,)), ((), ())), preferred_element_type=jnp.float32
            )
            scores = scores * (scales[0:1, :] * inverse)
            key_pos = source * local_len + lax.broadcasted_iota(jnp.int32, (1, local_len), 1)
            row = n * row_tile + lax.broadcasted_iota(jnp.int32, (row_tile, 1), 0)
            query_pos = prefix_len + ((row // rows_each) * n_ep + zed) * tokens + row % tokens
            scores = jnp.where(key_pos <= query_pos, scores, hidden_score)
            old = top[at, :]
            new = jnp.maximum(old, jnp.max(scores, axis=1, keepdims=True))
            exp_scores = jnp.exp(scores - new[:, :1])
            shrink = jnp.exp(old - new)
            total[at, :] = total[at, :] * shrink + jnp.sum(exp_scores, axis=1, keepdims=True)
            weighted = (exp_scores * scales[1:2, :]).astype(jnp.bfloat16)
            acc[at, :] = acc[at, :] * shrink + jnp.dot(
                weighted, kv[pl.ds(local_len, local_len), :], preferred_element_type=jnp.float32
            )
            top[at, :] = new
            return unused

        lax.fori_loop(first, last, one_tile, 0)

    attend(kv_ref.at[group], scale_ref.at[group], 0, 0)
    for q in range(1, copies):
        for c in arrivals[0, q]:
            c.wait_recv()
        attend(kv_all.at[0, q], scale_all.at[0, q], 0, q)
    for i in range(1, groups):
        for c in arrivals[i, 0]:
            c.wait_recv()
        for q in range(1, copies):
            arrivals[i, q] = send_kv(
                kv_all.at[i, 0],
                scale_all.at[i, 0],
                i,
                q,
                group * copies + (member + q) % copies,
            )
        attend(kv_all.at[i, 0], scale_all.at[i, 0], i, 0)
    tile_tokens = row_tile // heads
    waits = []
    for n in range(row_tiles):
        for i in range(1, groups):
            for q in range(1, copies):
                if n == 0:
                    for c in arrivals[i, q]:
                        c.wait_recv()
                attend(kv_all.at[i, q], scale_all.at[i, q], i, q, n, n + 1)
        for src in range(n * tile_tokens // tokens, (n + 1) * tile_tokens // tokens):
            for h in range(heads):
                at = pl.ds(src * rows_each + h * tokens, tokens)
                wide[pl.ds(src * tokens, tokens), pl.ds(h * head_dim, head_dim)] = (
                    acc[at, :] / total[at, :]
                )
        at = pl.ds(n * tile_tokens, tile_tokens)
        attn_all[zed, at, :] = wide[at, :].astype(jnp.bfloat16)
        for j in range(1, n_ep):
            waits.append(
                go(
                    attn_all.at[zed, at],
                    attn_all.at[zed, at],
                    attn_send.at[n, j],
                    attn_recv.at[n, j],
                    me,
                    (zed + j) % n_ep,
                )
            )
    for c in q_copies:
        c.wait_send()
    for pair in pending:
        for c in pair:
            c.wait_send()
    return waits


def layer_kernel(
    n_seq,
    n_ep,
    tokens,
    copies,
    heads,
    prefix_len,
    q_ref,
    kv_ref,
    scale_ref,
    out_weight_ref,
    residual_ref,
    gain_ref,
    mix_ref,
    gate_ref,
    up_ref,
    down_ref,
    hidden_ref,
    expert_ref,
    q_all,
    kv_all,
    scale_all,
    top,
    total,
    acc,
    tall,
    q_send,
    q_recv,
    kv_send,
    kv_recv,
    scale_send,
    scale_recv,
    own_sem,
    attn_all,
    mix_line,
    mix_all,
    mix_rows,
    out_w,
    gate_w,
    up_w,
    down_w,
    part_out,
    part_in,
    col_out,
    col_in,
    mine,
    gathered,
    rows,
    gate_acc,
    up_acc,
    active,
    partial,
    pair_in,
    plane_in,
    tail_out,
    tail_in,
    load_sem,
    local_sem,
    line_send,
    line_recv,
    mix_send,
    mix_recv,
    attn_send,
    attn_recv,
    part_send,
    part_recv,
    col_send,
    col_recv,
    a_send,
    a_recv,
    b_send,
    b_recv,
    c_send,
    c_recv,
    pair_send,
    pair_recv,
    plane_send,
    plane_recv,
    tail_send,
    tail_recv,
):
    me = lax.axis_index("seq")
    zed = lax.axis_index("ep")
    chips = n_seq // 2
    chip = me // 2
    core = me % 2
    other = chip * 2 + (1 - core)
    model = residual_ref.shape[1]
    half = model // 2
    bf16 = jnp.bfloat16
    f32 = jnp.float32

    loads = []
    for n, (src, dst) in enumerate(
        ((out_weight_ref, out_w), (gate_ref, gate_w), (up_ref, up_w), (down_ref, down_w))
    ):
        c = pltpu.make_async_copy(src, dst, load_sem.at[n])
        c.start()
        loads.append(c)

    barrier = pltpu.get_barrier_semaphore()
    for step in range(1, n_seq):
        pl.semaphore_signal(
            barrier, inc=1, device_id=device_at((me + step) % n_seq, zed), device_id_type=MESH
        )
    for step in range(1, n_ep):
        pl.semaphore_signal(
            barrier, inc=1, device_id=device_at(me, (zed + step) % n_ep), device_id_type=MESH
        )
    sends = []

    def go(*args):
        c = remote(*args)
        c.start()
        sends.append(c)
        return c

    waits = attention_part(
        go,
        n_seq,
        n_ep,
        copies,
        tokens,
        heads,
        prefix_len,
        q_ref,
        kv_ref,
        scale_ref,
        q_all,
        kv_all,
        scale_all,
        top,
        total,
        acc,
        tall,
        q_send,
        q_recv,
        kv_send,
        kv_recv,
        scale_send,
        scale_recv,
        own_sem,
        attn_all,
        attn_send,
        attn_recv,
    )
    line_keep = pltpu.make_async_copy(mix_ref, mix_line.at[zed], local_sem.at[3])
    line_keep.start()
    line_waits = [
        go(
            mix_ref,
            mix_line.at[zed],
            line_send.at[j],
            line_recv.at[j],
            me,
            (zed + j) % n_ep,
        )
        for j in range(1, n_ep)
    ]
    loads[0].wait()
    for c in waits:
        c.wait_recv()

    cols = out_w.shape[1]
    depth = attn_all.shape[2]
    part_waits = []
    attention = attn_all[...].reshape(n_ep * n_seq * tokens, depth)
    col_tile = 256
    for n in range(cols // col_tile):
        at = pl.ds(n * col_tile, col_tile)
        product = jnp.dot(attention, out_w[:, at], preferred_element_type=f32).reshape(
            n_ep, n_seq, tokens, col_tile
        )
        for s in range(n_seq):
            part_out[s, :, at] = product[:, s].reshape(n_ep * tokens, col_tile).astype(bf16)
    for step in range(1, n_seq):
        to = (me + step) % n_seq
        part_waits.append(
            go(
                part_out.at[to],
                part_in.at[step],
                part_send.at[step],
                part_recv.at[step],
                to,
                zed,
            )
        )
    line_keep.wait()
    for c in line_waits:
        c.wait_recv()
    mix_keep = pltpu.make_async_copy(mix_line, mix_all.at[me], local_sem.at[4])
    mix_keep.start()
    mix_waits = [
        go(
            mix_line,
            mix_all.at[me],
            mix_send.at[step],
            mix_recv.at[step],
            (me + step) % n_seq,
            zed,
        )
        for step in range(1, n_seq)
    ]
    for c in part_waits:
        c.wait_recv()
    summed = part_out[me].astype(f32)
    for step in range(1, n_seq):
        summed = summed + part_in[step].astype(f32)
    col_out[...] = summed.reshape(n_ep, tokens, cols)
    col_waits = []
    for j in range(1, n_ep):
        to = (zed + j) % n_ep
        col_waits.append(
            go(col_out.at[to], col_in.at[zed], col_send.at[j], col_recv.at[j], me, to)
        )
    keep = pltpu.make_async_copy(col_out.at[zed], col_in.at[zed], local_sem.at[1])
    keep.start()
    keep.wait()
    for c in col_waits:
        c.wait_recv()
    projected = jnp.concatenate([col_in[j] for j in range(n_ep)], axis=1)
    hidden = (residual_ref[...].astype(f32) + projected).astype(bf16)
    hidden_ref[...] = hidden
    wide = hidden.astype(f32)
    mean_square = jnp.mean(wide * wide, axis=1, keepdims=True)
    normed = wide * lax.rsqrt(mean_square + eps_norm) * gain_ref[...]
    mine[...] = jnp.concatenate([normed[:, :half], normed[:, half:]], axis=0).astype(bf16)

    keep = pltpu.make_async_copy(mine, gathered.at[core, chip, zed], local_sem.at[2])
    keep.start()
    spot = gathered.at[core, chip, zed]
    a_waits = {}
    b_waits = {}
    c_waits = []
    for j in range(1, n_ep):
        a_waits[j] = go(mine, spot, a_send.at[j], a_recv.at[j], me, (zed + j) % n_ep)

    def spread(src, at, j):
        for i in range(1, chips):
            to = ((chip + i) % chips) * 2 + core
            b_waits[i, j] = go(src, at, b_send.at[i, j], b_recv.at[i, j], to, zed)

    def across(src, at, i, j):
        c_waits.append(go(src, at, c_send.at[i, j], c_recv.at[i, j], other, zed))

    spread(mine, spot, 0)
    across(mine, spot, 0, 0)
    for j in range(1, n_ep):
        a_waits[j].wait_recv()
        at = gathered.at[core, chip, (zed + n_ep - j) % n_ep]
        spread(at, at, j)
        across(at, at, 0, j)
    mix_keep.wait()
    for c in mix_waits:
        c.wait_recv()
    expert = (me * n_ep + zed) // 2
    lane = lax.broadcasted_iota(jnp.int32, (1, mix_ref.shape[1]), 1)
    group_rows = n_ep * tokens
    for s in range(n_seq):
        weights = mix_all[s].reshape(group_rows, mix_ref.shape[1])
        weights = jnp.sum(jnp.where(lane == expert, weights, 0.0), axis=1, keepdims=True)
        at = pl.ds(((s % 2) * chips + s // 2) * group_rows, group_rows)
        mix_rows[at, :] = jnp.broadcast_to(weights, (group_rows, 128))
    for j in range(n_ep):
        for i in range(1, chips):
            b_waits[i, j].wait_recv()
            at = gathered.at[core, (chip + chips - i) % chips, (zed + n_ep - j) % n_ep]
            across(at, at, i, j)
    keep.wait()
    for c in c_waits:
        c.wait_recv()

    pairs = n_ep // 2

    def regroup(n, unused):
        blocks = gathered[n // (chips * pairs), (n // pairs) % chips, pl.ds((n % pairs) * 2, 2)]
        blocks = blocks.astype(f32)
        at = pl.ds(pl.multiple_of(n * 16, 16), 16)
        rows[at, pl.ds(0, half)] = jnp.concatenate(
            [blocks[0, :tokens], blocks[1, :tokens]], axis=0
        ).astype(bf16)
        rows[at, pl.ds(half, half)] = jnp.concatenate(
            [blocks[0, tokens:], blocks[1, tokens:]], axis=0
        ).astype(bf16)
        return unused

    lax.fori_loop(0, 2 * chips * pairs, regroup, 0)

    for c in loads[1:]:
        c.wait()
    gate_acc[...] = jnp.zeros_like(gate_acc)
    up_acc[...] = jnp.zeros_like(up_acc)
    depth_tile = 1024
    row_tile = 256
    count = rows.shape[0]

    def contract(n, unused):
        deep = pl.ds(pl.multiple_of(n * depth_tile, depth_tile), depth_tile)
        for r in range(count // row_tile):
            at = pl.ds(r * row_tile, row_tile)
            part = rows[at, deep]
            gate_acc[at, :] += jnp.dot(part, gate_w[deep, :], preferred_element_type=f32)
            up_acc[at, :] += jnp.dot(part, up_w[deep, :], preferred_element_type=f32)
        return unused

    lax.fori_loop(0, model // depth_tile, contract, 0)

    def activate(n, unused):
        at = pl.ds(pl.multiple_of(n * 64, 64), 64)
        gate = gate_acc[at, :]
        active[at, :] = (gate / (1.0 + jnp.exp(-gate)) * up_acc[at, :]).astype(bf16)
        return unused

    lax.fori_loop(0, count // 64, activate, 0)

    chunks = partial.shape[0]
    width = partial.shape[2]
    my_rows = count // 2
    chip_rows = n_ep * tokens
    pair_waits, plane_waits, tail_waits = {}, {}, {}

    def down(ch):
        deep = pl.ds(ch * width, width)
        for r in range(count // row_tile):
            at = pl.ds(r * row_tile, row_tile)
            for n in range(width // 256):
                deep = pl.ds(ch * width + n * 256, 256)
                y = jnp.dot(active[at, :], down_w[:, deep], preferred_element_type=f32)
                partial[ch, at, pl.ds(n * 256, 256)] = (y * mix_rows[at, :1]).astype(bf16)
        theirs = pl.ds(pl.multiple_of((1 - core) * my_rows, 16), my_rows)
        pair_waits[ch] = go(
            partial.at[ch, theirs],
            pair_in.at[ch],
            pair_send.at[ch],
            pair_recv.at[ch],
            other,
            zed,
        )

    def over_pair(ch):
        pair_waits[ch].wait_recv()
        ours = pl.ds(pl.multiple_of(core * my_rows, 16), my_rows)
        pair_in[ch] = (partial[ch, ours, :].astype(f32) + pair_in[ch].astype(f32)).astype(bf16)
        for i in range(1, chips):
            goal = (chip + i) % chips
            plane_waits[ch, i] = go(
                pair_in.at[ch, pl.ds(pl.multiple_of(goal * chip_rows, 16), chip_rows)],
                plane_in.at[ch, i - 1],
                plane_send.at[ch, i],
                plane_recv.at[ch, i],
                goal * 2 + core,
                zed,
            )

    def over_plane(ch):
        for i in range(1, chips):
            plane_waits[ch, i].wait_recv()
        ours = pl.ds(pl.multiple_of(chip * chip_rows, 16), chip_rows)
        value = pair_in[ch, ours, :].astype(f32)
        for i in range(1, chips):
            value = value + plane_in[ch, i - 1].astype(f32)
        for j in range(n_ep):
            block = value[j * tokens : (j + 1) * tokens]
            tail_out[ch, j] = jnp.concatenate(
                [block[:, : width // 2], block[:, width // 2 :]], axis=0
            ).astype(bf16)
        for j in range(1, n_ep):
            to = (zed + j) % n_ep
            tail_waits[ch, j] = go(
                tail_out.at[ch, to],
                tail_in.at[ch, j],
                tail_send.at[ch, j],
                tail_recv.at[ch, j],
                me,
                to,
            )

    def finish(ch):
        got = tail_out[ch, zed].astype(f32)
        value = jnp.concatenate([got[:tokens], got[tokens:]], axis=1)
        for j in range(1, n_ep):
            tail_waits[ch, j].wait_recv()
            got = tail_in[ch, j].astype(f32)
            value = value + jnp.concatenate([got[:tokens], got[tokens:]], axis=1)
        expert_ref[:, pl.ds(ch * width, width)] = value.astype(bf16)

    for step in range(chunks + 3):
        if step < chunks:
            down(step)
        if 0 <= step - 1 < chunks:
            over_pair(step - 1)
        if 0 <= step - 2 < chunks:
            over_plane(step - 2)
        if 0 <= step - 3 < chunks:
            finish(step - 3)
    for c in sends:
        c.wait_send()


def body(
    queries,
    key_codes,
    quantized_value_cache,
    key_scale,
    value_code_scale,
    out_weight,
    residual,
    norm_gain,
    route_ids,
    route_weight,
    w_gate,
    w_up,
    w_down,
):
    n_seq = lax.axis_size("seq")
    n_ep = lax.axis_size("ep")
    tokens, heads_all, head_dim = queries.shape
    local_len, kv_heads = key_scale.shape
    window_len = tokens * n_seq * n_ep
    prefix_len = local_len * n_seq - window_len
    heads = heads_all // n_seq
    copies = n_seq // kv_heads
    groups = n_seq // copies
    bf16, f32 = jnp.bfloat16, jnp.float32
    model = residual.shape[1]
    experts = n_seq * n_ep // 2

    mix = route_weight / jnp.sum(route_weight, axis=1, keepdims=True)
    grid = jnp.arange(experts, dtype=jnp.int32)
    dense = jnp.sum(
        jnp.where(route_ids[:, :, None] == grid[None, None, :], mix[:, :, None], 0.0), axis=1
    )
    lanes = -(-experts // 128) * 128
    dense = jnp.pad(dense, ((0, 0), (0, lanes - experts)))

    q_sorted = (
        queries.reshape(tokens, n_seq, heads, head_dim)
        .transpose(1, 2, 0, 3)
        .reshape(n_seq, heads * tokens, head_dim)
    )
    kv = jnp.concatenate(
        [key_codes.transpose(1, 0, 2), quantized_value_cache.transpose(1, 0, 2)], axis=1
    )
    scales = jnp.stack([key_scale.T, value_code_scale.T], axis=1).astype(f32)
    scales = jnp.pad(scales, ((0, 0), (0, 6), (0, 0)))
    q_rows = n_seq * heads * tokens
    vmem = pl.BlockSpec(memory_space=pltpu.VMEM)
    hbm = pl.BlockSpec(memory_space=pl.ANY)
    dma = pltpu.SemaphoreType.DMA
    cols = out_weight.shape[1]
    depth = out_weight.shape[0]
    wide = w_gate.shape[1]
    chips = n_seq // 2
    chunks = 2
    width = model // chunks
    return pl.pallas_call(
        functools.partial(
            layer_kernel, n_seq, n_ep, tokens, copies, heads, prefix_len
        ),
        out_shape=(
            jax.ShapeDtypeStruct((tokens, model), bf16),
            jax.ShapeDtypeStruct((tokens, model), bf16),
        ),
        in_specs=[vmem, vmem, vmem, hbm, vmem, vmem, vmem, hbm, hbm, hbm],
        out_specs=(vmem, vmem),
        scratch_shapes=[
            pltpu.VMEM((n_seq, heads * tokens, head_dim), bf16),
            pltpu.VMEM((groups, copies, 2 * local_len, head_dim), bf16),
            pltpu.VMEM((groups, copies, 8, local_len), f32),
            pltpu.VMEM((q_rows, head_dim), f32),
            pltpu.VMEM((q_rows, head_dim), f32),
            pltpu.VMEM((q_rows, head_dim), f32),
            pltpu.VMEM((n_seq * tokens, heads * head_dim), f32),
            dma((n_seq,)),
            dma((n_seq,)),
            dma((groups, copies)),
            dma((groups, copies)),
            dma((groups, copies)),
            dma((groups, copies)),
            dma,
            pltpu.VMEM((n_ep, n_seq * tokens, depth), bf16),
            pltpu.VMEM((n_ep, tokens, lanes), f32),
            pltpu.VMEM((n_seq, n_ep, tokens, lanes), f32),
            pltpu.VMEM((window_len, 128), f32),
            pltpu.VMEM((depth, cols), bf16),
            pltpu.VMEM((model, wide), bf16),
            pltpu.VMEM((model, wide), bf16),
            pltpu.VMEM((wide, model), bf16),
            pltpu.VMEM((n_seq, n_ep * tokens, cols), bf16),
            pltpu.VMEM((n_seq, n_ep * tokens, cols), bf16),
            pltpu.VMEM((n_ep, tokens, cols), f32),
            pltpu.VMEM((n_ep, tokens, cols), f32),
            pltpu.VMEM((2 * tokens, model // 2), bf16),
            pltpu.VMEM((2, chips, n_ep, 2 * tokens, model // 2), bf16),
            pltpu.VMEM((window_len, model), bf16),
            pltpu.VMEM((window_len, wide), f32),
            pltpu.VMEM((window_len, wide), f32),
            pltpu.VMEM((window_len, wide), bf16),
            pltpu.VMEM((chunks, window_len, width), bf16),
            pltpu.VMEM((chunks, window_len // 2, width), bf16),
            pltpu.VMEM((chunks, chips - 1, n_ep * tokens, width), bf16),
            pltpu.VMEM((chunks, n_ep, 2 * tokens, width // 2), bf16),
            pltpu.VMEM((chunks, n_ep, 2 * tokens, width // 2), bf16),
            dma((4,)),
            dma((5,)),
            dma((n_ep,)),
            dma((n_ep,)),
            dma((n_seq,)),
            dma((n_seq,)),
            dma((q_rows // 256, n_ep)),
            dma((q_rows // 256, n_ep)),
            dma((n_seq,)),
            dma((n_seq,)),
            dma((n_ep,)),
            dma((n_ep,)),
            dma((n_ep,)),
            dma((n_ep,)),
            dma((chips, n_ep)),
            dma((chips, n_ep)),
            dma((chips, n_ep)),
            dma((chips, n_ep)),
            dma((chunks,)),
            dma((chunks,)),
            dma((chunks, chips)),
            dma((chunks, chips)),
            dma((chunks, n_ep)),
            dma((chunks, n_ep)),
        ],
        compiler_params=pltpu.CompilerParams(
            collective_id=0, has_side_effects=True, vmem_limit_bytes=63 << 20
        ),
        name="layer",
    )(
        q_sorted,
        kv,
        scales,
        out_weight,
        residual,
        norm_gain.reshape(1, model),
        dense,
        w_gate,
        w_up,
        w_down,
    )


def solution(mesh):
    placed = (
        P(("grp", "seq", "ep"), None, None),
        P(("grp", "seq"), None, None),
        P(("grp", "seq"), None, None),
        P(("grp", "seq"), None),
        P(("grp", "seq"), None),
        P("seq", "ep"),
        P(("grp", "seq", "ep"), None),
        P(),
        P(("grp", "seq", "ep"), None),
        P(("grp", "seq", "ep"), None),
        P(None, ("seq", "ep")),
        P(None, ("seq", "ep")),
        P(("seq", "ep"), None),
    )
    return jax.shard_map(
        body,
        mesh=mesh,
        in_specs=placed,
        out_specs=(P(("grp", "seq", "ep"), None), P(("grp", "seq", "ep"), None)),
        check_vma=False,
    )
```
